32 devices in a mesh: groups: 2 (over y), node: 4 (over z), irrep: 4 (over x, core).
Axes of the slice: x: 2, y: 2, z: 4, core: 2. Of those that a mesh axis runs over, the one named last changes fastest.
Arguments:
- node_feats: bfloat16 [49, 128, 1024], P(None, 'irrep', ('groups', 'node')), parts along dimension 2, may hold values from -6 to 6
- cotangent: bfloat16 [49, 128, 1024], P(None, 'irrep', ('groups', 'node')), parts along dimension 2, may hold values from -6 to 6
- wigner: bfloat16 [235, 8192], P(None, ('groups', 'node')), parts along dimension 1, may hold values from -1.1953125 to 1.1953125
- sources: int32 [8192], P(('groups', 'node')), parts along dimension 0, may hold values from 0 to 511, as said below
- targets: int32 [8192], P(('groups', 'node')), parts along dimension 0, may hold values from 0 to 511, as said below
- counts: int32 [64], P(('groups', 'node')), parts along dimension 0, may hold values from 1 to 128, as said below
- first_zero: bfloat16 [896, 896], replicated, may hold values from -0.1875 to 0.1875
- first_one: bfloat16 [2, 768, 768], replicated, may hold values from -0.15625 to 0.15625
- first_two: bfloat16 [2, 640, 640], replicated, may hold values from -0.15625 to 0.15625
- second_zero: bfloat16 [896, 896], replicated, may hold values from -0.1875 to 0.1875
- second_one: bfloat16 [2, 768, 768], replicated, may hold values from -0.15625 to 0.15625
- second_two: bfloat16 [2, 640, 640], replicated, may hold values from -0.15625 to 0.15625
Outputs:
- node_update: bfloat16 [49, 128, 1024], P(None, 'irrep', ('groups', 'node')), parts along dimension 2
- source_grad: float32 [49, 128, 1024], P(None, 'irrep', ('groups', 'node')), parts along dimension 2
The draws below stay inside these ranges and needn't reach their ends.
There are 2 independent parts, one for each index of `groups`. The reference program is written for one: setup_inputs(seed, part) draws one part's arguments, and reference() takes and returns one part's arrays. A program takes and returns all parts, laid end to end along the dimension named above; an argument that names none is the same for every part. Nothing has to cross between parts.
Inputs may be any that keep to these rules, and one draw needn't show every extreme that they name: `targets`: edge slot e belongs to shard s = e // 1024, and its destination atom lies in s * 128 .. s * 128 + 127. `sources`: of the 1024 edge slots of one shard, at most 512 have source atoms in one node shard's range of 128 atoms, and in every shard that most is reached. Block b's live edges sit in its first counts[b] slots; the other slots hold valid indices and are ignored. The first block of every shard is full, the second holds one live edge.
All inputs are finite; a program needn't handle non-finite values.
Results may differ from the reference program's by a relative error of at most 0.0071.
Values may be sent and summed in bfloat16 or wider, within the bound.
A program may use at most 192 MiB of HBM per device.

```python
import jax
import jax.numpy as jnp
from jax import lax

CH = 128
LMAX = 6
MMAX = 2
A_DEV = 128
NBLK = 8
BLOCK = 128
COEF = 49
WIG = 235
ATOMS = 512
EDGES = 4096
NB_ALL = 32
N_NODE = 4


def draw_sources(key, part):
    key = jax.random.fold_in(key, 37)
    perm_key, atom_key = jax.random.split(key)
    shard_edges = NBLK * BLOCK
    share_size = shard_edges // N_NODE
    slot_ids = jnp.arange(shard_edges, dtype=jnp.int32)
    group_ids = slot_ids // share_size
    within = slot_ids % share_size
    moved = ((group_ids == 1) | (group_ids == N_NODE // 2)) & (within >= share_size // 2)
    offsets = jnp.where(moved, 0, group_ids).astype(jnp.int32)
    shuffles = jax.vmap(lambda sub_key: jax.random.permutation(sub_key, shard_edges))(jax.random.split(perm_key, N_NODE))
    shard_ids = jnp.arange(N_NODE, dtype=jnp.int32)[:, None]
    owners = (shard_ids + offsets[shuffles]) % N_NODE
    atoms = owners * A_DEV + jax.random.randint(atom_key, (N_NODE, shard_edges), 0, A_DEV, dtype=jnp.int32)
    return atoms.reshape(EDGES).astype(jnp.int32)


def draw_targets(key, part):
    key = jax.random.fold_in(key, 11)
    edge_ids = jnp.arange(EDGES, dtype=jnp.int32)
    shard_ids = edge_ids // (NBLK * BLOCK)
    return (shard_ids * A_DEV + jax.random.randint(key, (EDGES,), 0, A_DEV, dtype=jnp.int32)).astype(jnp.int32)


def draw_counts(key, part):
    key = jax.random.fold_in(key, 23)
    level_key, drop_key = jax.random.split(key)
    block_ids = jnp.arange(NB_ALL, dtype=jnp.int32)
    levels = jax.random.randint(level_key, (NB_ALL // NBLK,), BLOCK // 3, BLOCK + 1, dtype=jnp.int32)
    ceiling = levels[block_ids // NBLK]
    drawn_counts = ceiling - jax.random.randint(drop_key, (NB_ALL,), 0, ceiling // 2 + 1, dtype=jnp.int32)
    drawn_counts = jnp.where(block_ids % NBLK == 1, 1, drawn_counts)
    return jnp.where(block_ids % NBLK == 0, BLOCK, drawn_counts).astype(jnp.int32)


def level_of(stream_key, dims, cuts, smallest, high):
    loudness = 1.0
    for axis_at, blocks in cuts:
        heights = jax.random.uniform(jax.random.fold_in(jax.random.fold_in(stream_key, 6), axis_at), (blocks,), jnp.float32, smallest / len(cuts), high / len(cuts))
        loudness = loudness * jnp.repeat(jnp.exp(heights), dims[axis_at] // blocks).reshape((-1,) + (1,) * (len(dims) - 1 - axis_at))
    return loudness


def normal_values(rng, extent, width, most, shards=(), kind=jnp.bfloat16):
    values = jax.random.normal(rng, extent, jnp.float32) * width
    if len(shards) > 0:
        values = level_of(rng, extent, shards, -0.22, 0.18) * values
    return jnp.clip(values, min=-most, max=most).astype(kind)


def setup_inputs(seed: int = 0, part: int = 0) -> dict:
    key_of = jax.random.split(jax.random.key(seed), 13)
    part_splits = jax.random.split(jax.random.fold_in(key_of[12], part), 13)
    node_feats = normal_values(part_splits[0], (COEF, CH, ATOMS), 1.0, 6.0, ((1, 4), (2, 4)))
    cotangent = normal_values(part_splits[1], (COEF, CH, ATOMS), 1.0, 6.0, ((1, 4), (2, 4)))
    wigner = normal_values(part_splits[2], (WIG, EDGES), 0.3, 1.1953125, ((1, 4),))
    sources = draw_sources(jax.random.fold_in(jax.random.fold_in(key_of[12], part), 71), part)
    targets = draw_targets(jax.random.fold_in(jax.random.fold_in(key_of[12], part), 71), part)
    counts = draw_counts(jax.random.fold_in(jax.random.fold_in(key_of[12], part), 71), part)
    first_zero = normal_values(key_of[6], ((LMAX + 1) * CH, (LMAX + 1) * CH), ((LMAX + 1) * CH) ** -0.5, 0.1875)
    first_one = normal_values(key_of[7], (2, LMAX * CH, LMAX * CH), (2 * LMAX * CH) ** -0.5, 0.15625)
    first_two = normal_values(key_of[8], (2, (LMAX - 1) * CH, (LMAX - 1) * CH), (2 * (LMAX - 1) * CH) ** -0.5, 0.15625)
    second_zero = normal_values(key_of[9], ((LMAX + 1) * CH, (LMAX + 1) * CH), ((LMAX + 1) * CH) ** -0.5, 0.1875)
    second_one = normal_values(key_of[10], (2, LMAX * CH, LMAX * CH), (2 * LMAX * CH) ** -0.5, 0.15625)
    second_two = normal_values(key_of[11], (2, (LMAX - 1) * CH, (LMAX - 1) * CH), (2 * (LMAX - 1) * CH) ** -0.5, 0.15625)
    return {"node_feats": node_feats, "cotangent": cotangent, "wigner": wigner, "sources": sources, "targets": targets, "counts": counts, "first_zero": first_zero, "first_one": first_one, "first_two": first_two, "second_zero": second_zero, "second_one": second_one, "second_two": second_two}


edge_scale = 0.5


def frame_row(degree, order_num):
    top_rows = LMAX + 1
    if order_num == 0:
        return degree
    if order_num == 1:
        return top_rows + degree - 1
    if order_num == -1:
        return top_rows + LMAX + degree - 1
    if order_num == 2:
        return top_rows + 2 * LMAX + degree - 2
    return top_rows + 3 * LMAX - 1 + degree - 2


def rotate_in(values, wigner):
    frame_rows = {}
    offset = 0
    for degree in range(LMAX + 1):
        keep_count = min(degree, MMAX)
        col_count = 2 * degree + 1
        row_total = 2 * keep_count + 1
        rot_block = wigner[offset:offset + row_total * col_count].astype(jnp.float32)
        offset += row_total * col_count
        deg_part = values[degree * degree:degree * degree + col_count].astype(jnp.float32)
        for row_index in range(row_total):
            summed = rot_block[row_index * col_count][None, :] * deg_part[0]
            for col_index in range(1, col_count):
                summed = summed + rot_block[row_index * col_count + col_index][None, :] * deg_part[col_index]
            frame_rows[frame_row(degree, row_index - keep_count)] = summed
    return jnp.stack([frame_rows[position] for position in range(len(frame_rows))])


def rotate_out(frame, wigner):
    degree_rows = []
    offset = 0
    for degree in range(LMAX + 1):
        keep_count = min(degree, MMAX)
        col_count = 2 * degree + 1
        row_total = 2 * keep_count + 1
        rot_block = wigner[offset:offset + row_total * col_count].astype(jnp.float32)
        offset += row_total * col_count
        frame_list = [frame[frame_row(degree, row_index - keep_count)].astype(jnp.float32) for row_index in range(row_total)]
        for col_index in range(col_count):
            summed = rot_block[col_index][None, :] * frame_list[0]
            for row_index in range(1, row_total):
                summed = summed + rot_block[row_index * col_count + col_index][None, :] * frame_list[row_index]
            degree_rows.append(summed)
    return jnp.stack(degree_rows)


def apply_matrix(matrix, operand, transposed):
    if transposed:
        return lax.dot_general(matrix, operand, (((0,), (0,)), ((), ())), preferred_element_type=jnp.float32)
    return jnp.dot(matrix, operand, preferred_element_type=jnp.float32)


def mix_orders(weights, frame, transposed):
    w_zero, w_one, w_two = weights
    channels = frame.shape[1]
    edge_count = frame.shape[2]
    top_rows = LMAX + 1

    def flatten_rows(row_start, row_stop):
        return frame[row_start:row_stop].reshape((row_stop - row_start) * channels, edge_count)

    zero_out = apply_matrix(w_zero, flatten_rows(0, top_rows), transposed)
    out_list = [zero_out.reshape(top_rows, channels, edge_count)]
    row_start = top_rows
    for order_num in (1, 2):
        matrix = w_one if order_num == 1 else w_two
        order_rows = LMAX + 1 - order_num
        paired = jnp.concatenate([flatten_rows(row_start, row_start + order_rows), flatten_rows(row_start + order_rows, row_start + 2 * order_rows)], axis=1)
        real_part = apply_matrix(matrix[0], paired, transposed)
        imag_part = apply_matrix(matrix[1], paired, transposed)
        if transposed:
            plus_part = real_part[:, :edge_count] + imag_part[:, edge_count:]
            minus_part = real_part[:, edge_count:] - imag_part[:, :edge_count]
        else:
            plus_part = real_part[:, :edge_count] - imag_part[:, edge_count:]
            minus_part = imag_part[:, :edge_count] + real_part[:, edge_count:]
        out_list.append(plus_part.reshape(order_rows, channels, edge_count))
        out_list.append(minus_part.reshape(order_rows, channels, edge_count))
        row_start += 2 * order_rows
    return jnp.concatenate(out_list, axis=0)


def gate_forward(hidden):
    scalar = hidden[0]
    gate_sig = jax.nn.sigmoid(scalar)
    return jnp.concatenate([(scalar * gate_sig)[None], hidden[1:] * gate_sig[None]], axis=0).astype(jnp.bfloat16)


def gate_backward(incoming, hidden):
    scalar = hidden[0]
    gate_sig = jax.nn.sigmoid(scalar)
    first_row = incoming[0] * gate_sig * (1.0 + scalar * (1.0 - gate_sig)) + gate_sig * (1.0 - gate_sig) * jnp.sum(incoming[1:] * hidden[1:], axis=0)
    return jnp.concatenate([first_row[None], incoming[1:] * gate_sig[None]], axis=0).astype(jnp.bfloat16)


def edge_work(first, second, edge_frame, back_seed):
    hidden = mix_orders(first, edge_frame, False)
    gated = gate_forward(hidden)
    message = mix_orders(second, gated, False).astype(jnp.bfloat16)
    back_gate = mix_orders(second, back_seed, True)
    back_hidden = gate_backward(back_gate, hidden)
    back_frame = mix_orders(first, back_hidden, True).astype(jnp.bfloat16)
    return message, back_frame


def reference(node_feats, cotangent, wigner, sources, targets, counts, first_zero, first_one, first_two, second_zero, second_one, second_two):
    first = (first_zero, first_one, first_two)
    second = (second_zero, second_one, second_two)
    shard_edges = NBLK * BLOCK
    atom_count = A_DEV * N_NODE
    coef_count = node_feats.shape[0]
    channels = node_feats.shape[1]

    def shard_step(grad_total, shard_index):
        edge_start = (shard_index * shard_edges).astype(jnp.int32)
        shard_src = lax.dynamic_slice_in_dim(sources, edge_start, shard_edges)
        shard_dst = lax.dynamic_slice_in_dim(targets, edge_start, shard_edges)
        shard_wig = lax.dynamic_slice_in_dim(wigner, edge_start, shard_edges, 1)
        live_counts = lax.dynamic_slice_in_dim(counts, (shard_index * NBLK).astype(jnp.int32), NBLK)
        live_mask = (jnp.arange(BLOCK, dtype=jnp.int32)[None, :] < live_counts[:, None]).reshape(shard_edges).astype(jnp.bfloat16)
        source_rows = jnp.take(node_feats, shard_src, axis=2)
        seed_rows = jnp.take(cotangent, shard_dst, axis=2) * live_mask
        edge_frame = rotate_in(source_rows, shard_wig).astype(jnp.bfloat16)
        back_seed = rotate_in(seed_rows, shard_wig).astype(jnp.bfloat16)
        message, back_frame = edge_work(first, second, edge_frame, back_seed)
        sent_rows = rotate_out(message, shard_wig).astype(jnp.bfloat16)
        returned = rotate_out(back_frame, shard_wig).astype(jnp.bfloat16)
        local_dst = (shard_dst - shard_index * A_DEV).astype(jnp.int32)
        gathered = jnp.zeros((coef_count, channels, A_DEV), jnp.float32).at[:, :, local_dst].add(sent_rows.astype(jnp.float32) * live_mask.astype(jnp.float32))
        node_part = (edge_scale * gathered).astype(jnp.bfloat16)
        spread = jnp.zeros((coef_count, channels, atom_count), jnp.float32).at[:, :, shard_src].add(returned.astype(jnp.float32))
        return grad_total + edge_scale * spread, node_part

    grad_total, updates = lax.scan(shard_step, jnp.zeros((coef_count, channels, atom_count), jnp.float32), jnp.arange(N_NODE, dtype=jnp.int32))
    node_update = jnp.transpose(updates, (1, 2, 0, 3)).reshape(coef_count, channels, atom_count)
    return node_update, grad_total
```

```python
import functools

import jax
import jax.numpy as jnp
from jax import lax
from jax.experimental import pallas as pl
from jax.experimental.pallas import tpu as pltpu
from jax.sharding import PartitionSpec as P

LMAX = 6
MMAX = 2
COEF = (LMAX + 1) ** 2
EDGE_SCALE = 0.5
F32 = jnp.float32
BF16 = jnp.bfloat16
MESH = pl.DeviceIdType.MESH
VMEM_LIMIT = 60 * 1024 * 1024

BASE = [0]
WOFF = [0]
for _l in range(LMAX + 1):
    _rows = 2 * min(_l, MMAX) + 1
    BASE.append(BASE[-1] + _rows)
    WOFF.append(WOFF[-1] + _rows * (2 * _l + 1))
ROWS = BASE[-1]

PARTS = ((0, 4), (4, 6), (6, 7))


def frow(degree, order):
    return BASE[degree] + order + min(degree, MMAX)


def coef_rows(part):
    low, high = PARTS[part]
    return low * low, high * high - low * low


def frame_rows(part):
    low, high = PARTS[part]
    return BASE[low], BASE[high] - BASE[low]


def rotate_in(src, dst, wig, degrees, channels, edges, wig_base):
    halves = channels // 16

    def body(step, carry):
        tile = step // halves
        half = step % halves
        lanes = pl.ds(pl.multiple_of(tile * 128, 128), 128)
        wig_lanes = pl.ds(pl.multiple_of(wig_base + tile * 128, 128), 128)
        chans = pl.ds(pl.multiple_of(half * 16, 16), 16)
        for degree in degrees:
            cols = 2 * degree + 1
            parts = [src[degree * degree + c, chans, lanes].astype(F32) for c in range(cols)]
            for r in range(2 * min(degree, MMAX) + 1):
                at = WOFF[degree] + r * cols
                total = wig[at : at + 1, wig_lanes] * parts[0]
                for c in range(1, cols):
                    total = total + wig[at + c : at + c + 1, wig_lanes] * parts[c]
                dst[BASE[degree] + r, chans, lanes] = total.astype(BF16)
        return carry

    lax.fori_loop(0, (edges // 128) * halves, body, 0)


def rotate_out(src, dst, wig, degrees, channels, edges, wig_base):
    halves = channels // 16

    def body(step, carry):
        tile = step // halves
        half = step % halves
        lanes = pl.ds(pl.multiple_of(tile * 128, 128), 128)
        wig_lanes = pl.ds(pl.multiple_of(wig_base + tile * 128, 128), 128)
        chans = pl.ds(pl.multiple_of(half * 16, 16), 16)
        for degree in degrees:
            cols = 2 * degree + 1
            count = 2 * min(degree, MMAX) + 1
            parts = [src[BASE[degree] + r, chans, lanes].astype(F32) for r in range(count)]
            for c in range(cols):
                at = WOFF[degree] + c
                total = wig[at : at + 1, wig_lanes] * parts[0]
                for r in range(1, count):
                    at = WOFF[degree] + r * cols + c
                    total = total + wig[at : at + 1, wig_lanes] * parts[r]
                dst[degree * degree + c, chans, lanes] = total.astype(BF16)
        return carry

    lax.fori_loop(0, (edges // 128) * halves, body, 0)


def dot_nn(a, b):
    return jnp.dot(a, b, preferred_element_type=F32)


def dot_tn(a, b):
    return lax.dot_general(a, b, (((0,), (0,)), ((), ())), preferred_element_type=F32)


def dot_nt(a, b):
    return lax.dot_general(a, b, (((1,), (1,)), ((), ())), preferred_element_type=F32)


def mix(weights, frame, out, transposed, dtype):
    zero, one, two = weights
    width, share = frame.shape[1], frame.shape[2]
    dot = dot_tn if transposed else dot_nn
    rows = jnp.concatenate([frame[frow(l, 0)] for l in range(LMAX + 1)], axis=0)
    res = dot(zero[...], rows)
    for l in range(LMAX + 1):
        out[frow(l, 0)] = res[l * width : (l + 1) * width].astype(dtype)
    for order, mat in ((1, one), (2, two)):
        degrees = range(order, LMAX + 1)
        rows = jnp.concatenate(
            [
                jnp.concatenate([frame[frow(l, order)], frame[frow(l, -order)]], axis=1)
                for l in degrees
            ],
            axis=0,
        )
        real = dot(mat[0], rows)
        imag = dot(mat[1], rows)
        if transposed:
            plus = real[:, :share] + imag[:, share:]
            minus = real[:, share:] - imag[:, :share]
        else:
            plus = real[:, :share] - imag[:, share:]
            minus = imag[:, :share] + real[:, share:]
        for at, l in enumerate(degrees):
            out[frow(l, order)] = plus[at * width : (at + 1) * width].astype(dtype)
            out[frow(l, -order)] = minus[at * width : (at + 1) * width].astype(dtype)


def kernel(
    n_node,
    n_irrep,
    node_hbm,
    cot_hbm,
    wig_in,
    sources,
    dests,
    fz_hbm,
    fo_hbm,
    ft_hbm,
    sz_hbm,
    so_hbm,
    st_hbm,
    update,
    grad,
    fz,
    fo,
    ft,
    sz,
    so,
    st,
    wig,
    src_table,
    dst_table,
    nodes_all,
    cot_all,
    src_rows,
    seed_rows,
    frame_out,
    frame_in,
    seed_frame,
    hidden,
    back_gate,
    gated,
    message,
    back_hidden,
    back_frame,
    back_in,
    sent_rows,
    ret_rows,
    upd_out,
    upd_in,
    grad_out,
    grad_in,
    load_sem,
    local_sem,
    node_send,
    node_recv,
    cot_send,
    cot_recv,
    fr_send,
    fr_recv,
    bk_send,
    bk_recv,
    up_send,
    up_recv,
    gr_send,
    gr_recv,
):
    group = lax.axis_index("groups")
    me_n = lax.axis_index("node")
    me_i = lax.axis_index("irrep")
    chans, atoms = node_hbm.shape[1], node_hbm.shape[2]
    width = chans * n_irrep
    edges = sources.shape[1]
    share = edges // n_irrep
    all_atoms = atoms * n_node

    def node_peer(k):
        return (group, lax.rem(me_n + k, n_node), me_i)

    def irrep_peer(k):
        return (group, me_n, lax.rem(me_i + k, n_irrep))

    loads = [
        pltpu.make_async_copy(a, b, load_sem.at[i])
        for i, (a, b) in enumerate(
            ((fz_hbm, fz), (fo_hbm, fo), (ft_hbm, ft), (sz_hbm, sz), (so_hbm, so), (st_hbm, st))
        )
    ]

    barrier = pltpu.get_barrier_semaphore()
    for k in range(1, n_node):
        pl.semaphore_signal(barrier, inc=1, device_id=node_peer(k), device_id_type=MESH)
    for k in range(1, n_irrep):
        pl.semaphore_signal(barrier, inc=1, device_id=irrep_peer(k), device_id_type=MESH)
    pl.semaphore_wait(barrier, n_node + n_irrep - 2)

    sends = []

    def remote(src, dst, send, recv, peer):
        copy = pltpu.make_async_remote_copy(
            src_ref=src,
            dst_ref=dst,
            send_sem=send,
            recv_sem=recv,
            device_id=peer,
            device_id_type=MESH,
        )
        copy.start()
        sends.append(copy)
        return copy

    my_atoms = pl.ds(pl.multiple_of(me_n * atoms, atoms), atoms)
    my_chans = pl.ds(pl.multiple_of(me_i * chans, chans), chans)
    my_share = pl.multiple_of(me_i * share, share)
    my_edges = pl.ds(my_share, share)

    node_copies = []
    for part in range(len(PARTS)):
        at, count = coef_rows(part)
        node_copies.append(
            [
                remote(
                    node_hbm.at[pl.ds(at, count)],
                    nodes_all.at[pl.ds(at, count), :, my_atoms],
                    node_send.at[part, k - 1],
                    node_recv.at[part, k - 1],
                    node_peer(k),
                )
                for k in range(1, n_node)
            ]
        )
    cot_copies = [
        remote(
            cot_hbm,
            cot_all.at[:, my_chans, :],
            cot_send.at[k - 1],
            cot_recv.at[k - 1],
            irrep_peer(k),
        )
        for k in range(1, n_irrep)
    ]
    own_node = pltpu.make_async_copy(node_hbm, nodes_all.at[:, :, my_atoms], local_sem.at[0])
    own_cot = pltpu.make_async_copy(cot_hbm, cot_all.at[:, my_chans, :], local_sem.at[1])
    own_node.start()
    own_cot.start()
    for copy in loads:
        copy.start()

    wig[...] = wig_in[...].astype(F32)

    def fill(i, carry):
        at = pl.multiple_of(i * 128, 128)
        rows = lax.broadcasted_iota(jnp.int32, (128, edges), 0) + i * 128
        src_table[pl.ds(at, 128), :] = jnp.where(rows == sources[...], 1.0, 0.0).astype(BF16)
        return carry

    lax.fori_loop(0, all_atoms // 128, fill, 0)
    rows = lax.broadcasted_iota(jnp.int32, (atoms, share), 0)
    dst_table[...] = jnp.where(rows == dests[:, my_edges], 1.0, 0.0).astype(BF16)

    own_cot.wait()
    for copy in cot_copies:
        copy.wait_recv()

    def seed(i, carry):
        cot = cot_all[pl.ds(i * 7, 7)].reshape(7 * width, atoms)
        got = dot_nn(cot, dst_table[...]).astype(BF16)
        seed_rows[pl.ds(i * 7, 7)] = got.reshape(7, width, share)
        return carry

    lax.fori_loop(0, COEF // 7, seed, 0)
    rotate_in(seed_rows, seed_frame, wig, range(LMAX + 1), width, share, my_share)

    own_node.wait()
    frame_copies = []
    own_frames = []
    for part in range(len(PARTS)):
        for copy in node_copies[part]:
            copy.wait_recv()
        at, count = coef_rows(part)

        def gather(i, carry, at=at, count=count):
            lanes = pl.ds(pl.multiple_of(i * 256, 256), 256)
            tab = nodes_all[pl.ds(at, count)].reshape(count * chans, all_atoms)
            got = dot_nn(tab, src_table[:, lanes]).astype(BF16)
            src_rows[pl.ds(at, count), :, lanes] = got.reshape(count, chans, 256)
            return carry

        lax.fori_loop(0, edges // 256, gather, 0)
        rotate_in(src_rows, frame_out, wig, range(*PARTS[part]), chans, edges, 0)
        at, count = frame_rows(part)
        sent = []
        for k in range(1, n_irrep):
            peer = lax.rem(me_i + k, n_irrep)
            lanes = pl.ds(pl.multiple_of(peer * share, share), share)
            sent.append(
                remote(
                    frame_out.at[pl.ds(at, count), :, lanes],
                    frame_in.at[pl.ds(at, count), my_chans, :],
                    fr_send.at[part, k - 1],
                    fr_recv.at[part, k - 1],
                    irrep_peer(k),
                )
            )
        frame_copies.append(sent)
        own = pltpu.make_async_copy(
            frame_out.at[pl.ds(at, count), :, my_edges],
            frame_in.at[pl.ds(at, count), my_chans, :],
            local_sem.at[2 + part],
        )
        own.start()
        own_frames.append(own)

    for copy in loads:
        copy.wait()
    first = (fz, fo, ft)
    second = (sz, so, st)
    mix(second, seed_frame, back_gate, True, F32)
    for part in range(len(PARTS)):
        own_frames[part].wait()
        for copy in frame_copies[part]:
            copy.wait_recv()
    mix(first, frame_in, hidden, False, F32)

    def gate(i, carry):
        rows16 = pl.ds(pl.multiple_of(i * 16, 16), 16)
        s = hidden[0, rows16, :]
        g = jax.nn.sigmoid(s)
        total = jnp.zeros_like(s)
        gated[0, rows16, :] = (s * g).astype(BF16)
        for r in range(1, ROWS):
            h = hidden[r, rows16, :]
            b = back_gate[r, rows16, :]
            total = total + b * h
            gated[r, rows16, :] = (h * g).astype(BF16)
            back_hidden[r, rows16, :] = (b * g).astype(BF16)
        top = back_gate[0, rows16, :] * g * (1.0 + s * (1.0 - g)) + g * (1.0 - g) * total
        back_hidden[0, rows16, :] = top.astype(BF16)
        return carry

    lax.fori_loop(0, width // 16, gate, 0)

    mix(first, back_hidden, back_frame, True, BF16)
    back_copies = []
    own_backs = []
    for part in range(len(PARTS)):
        at, count = frame_rows(part)
        sent = []
        for k in range(1, n_irrep):
            peer = lax.rem(me_i + k, n_irrep)
            theirs = pl.ds(pl.multiple_of(peer * chans, chans), chans)
            sent.append(
                remote(
                    back_frame.at[pl.ds(at, count), theirs, :],
                    back_in.at[pl.ds(at, count), :, my_edges],
                    bk_send.at[part, k - 1],
                    bk_recv.at[part, k - 1],
                    irrep_peer(k),
                )
            )
        back_copies.append(sent)
        own = pltpu.make_async_copy(
            back_frame.at[pl.ds(at, count), my_chans, :],
            back_in.at[pl.ds(at, count), :, my_edges],
            local_sem.at[2 + len(PARTS) + part],
        )
        own.start()
        own_backs.append(own)

    mix(second, gated, message, False, BF16)
    rotate_out(message, sent_rows, wig, range(LMAX + 1), width, share, my_share)

    def aggregate(i, carry):
        rows7 = sent_rows[pl.ds(i * 7, 7)].reshape(7 * width, share)
        got = dot_nt(rows7, dst_table[...]).astype(BF16)
        upd_out[pl.ds(i * 7, 7)] = got.reshape(7, width, atoms)
        return carry

    lax.fori_loop(0, COEF // 7, aggregate, 0)
    upd_copies = []
    for k in range(1, n_irrep):
        peer = lax.rem(me_i + k, n_irrep)
        theirs = pl.ds(pl.multiple_of(peer * chans, chans), chans)
        upd_copies.append(
            remote(
                upd_out.at[:, theirs, :],
                upd_in.at[k - 1],
                up_send.at[k - 1],
                up_recv.at[k - 1],
                irrep_peer(k),
            )
        )

    grad_copies = []
    for part in range(len(PARTS)):
        own_backs[part].wait()
        for copy in back_copies[part]:
            copy.wait_recv()
        rotate_out(back_in, ret_rows, wig, range(*PARTS[part]), chans, edges, 0)
        at, count = coef_rows(part)

        def spread(i, carry, at=at, count=count):
            tab = src_table[pl.ds(pl.multiple_of(i * 2 * atoms, 2 * atoms), 2 * atoms), :]
            got = dot_nt(ret_rows[pl.ds(at, count)].reshape(count * chans, edges), tab)
            got = got.astype(BF16)
            for j in range(2):
                piece = got[:, j * atoms : (j + 1) * atoms].reshape(count, chans, atoms)
                grad_out[2 * i + j, pl.ds(at, count)] = piece
            return carry

        lax.fori_loop(0, n_node // 2, spread, 0)
        sent = []
        for k in range(1, n_node):
            peer = lax.rem(me_n + k, n_node)
            sent.append(
                remote(
                    grad_out.at[peer, pl.ds(at, count)],
                    grad_in.at[k - 1, pl.ds(at, count)],
                    gr_send.at[part, k - 1],
                    gr_recv.at[part, k - 1],
                    node_peer(k),
                )
            )
        grad_copies.append(sent)

    for copy in upd_copies:
        copy.wait_recv()

    def finish_update(i, carry):
        total = upd_out[i, my_chans, :].astype(F32)
        for k in range(n_irrep - 1):
            total = total + upd_in[k, i].astype(F32)
        update[i] = (EDGE_SCALE * total).astype(BF16)
        return carry

    lax.fori_loop(0, COEF, finish_update, 0)

    for part in range(len(PARTS)):
        for copy in grad_copies[part]:
            copy.wait_recv()
        at, count = coef_rows(part)

        def finish_grad(i, carry):
            total = grad_out[me_n, i].astype(F32)
            for k in range(n_node - 1):
                total = total + grad_in[k, i].astype(F32)
            grad[i] = EDGE_SCALE * total
            return carry

        lax.fori_loop(at, at + count, finish_grad, 0)

    for copy in sends:
        copy.wait_send()


def local(
    n_node,
    n_irrep,
    node_feats,
    cotangent,
    wigner,
    sources,
    targets,
    counts,
    first_zero,
    first_one,
    first_two,
    second_zero,
    second_one,
    second_two,
):
    coefs, chans, atoms = node_feats.shape
    edges = sources.shape[0]
    share = edges // n_irrep
    width = chans * n_irrep
    blocks = counts.shape[0]
    slot = jnp.arange(edges // blocks, dtype=jnp.int32)
    live = (slot[None, :] < counts[:, None]).reshape(edges)
    dests = jnp.where(live, targets - lax.axis_index("node") * atoms, -1).reshape(1, edges)
    weights = (first_zero, first_one, first_two, second_zero, second_one, second_two)
    parts = len(PARTS)
    vmem = pltpu.VMEM
    dma = pltpu.SemaphoreType.DMA
    frame = (ROWS, width, share)
    scratch = [vmem(w.shape, BF16) for w in weights] + [
        vmem(wigner.shape, F32),
        vmem((atoms * n_node, edges), BF16),
        vmem((atoms, share), BF16),
        vmem((coefs, chans, atoms * n_node), BF16),
        vmem((coefs, width, atoms), BF16),
        vmem((coefs, chans, edges), BF16),
        vmem((coefs, width, share), BF16),
        vmem((ROWS, chans, edges), BF16),
        vmem(frame, BF16),
        vmem(frame, BF16),
        vmem(frame, F32),
        vmem(frame, F32),
        vmem(frame, BF16),
        vmem(frame, BF16),
        vmem(frame, BF16),
        vmem(frame, BF16),
        vmem((ROWS, chans, edges), BF16),
        vmem((coefs, width, share), BF16),
        vmem((coefs, chans, edges), BF16),
        vmem((coefs, width, atoms), BF16),
        vmem((n_irrep - 1, coefs, chans, atoms), BF16),
        vmem((n_node, coefs, chans, atoms), BF16),
        vmem((n_node - 1, coefs, chans, atoms), BF16),
        dma((len(weights),)),
        dma((2 + 2 * parts,)),
        dma((parts, n_node - 1)),
        dma((parts, n_node - 1)),
        dma((n_irrep - 1,)),
        dma((n_irrep - 1,)),
        dma((parts, n_irrep - 1)),
        dma((parts, n_irrep - 1)),
        dma((parts, n_irrep - 1)),
        dma((parts, n_irrep - 1)),
        dma((n_irrep - 1,)),
        dma((n_irrep - 1,)),
        dma((parts, n_node - 1)),
        dma((parts, n_node - 1)),
    ]
    hbm = pl.BlockSpec(memory_space=pl.ANY)
    inside = pl.BlockSpec(memory_space=pltpu.VMEM)
    return pl.pallas_call(
        functools.partial(kernel, n_node, n_irrep),
        out_shape=(
            jax.ShapeDtypeStruct(node_feats.shape, BF16),
            jax.ShapeDtypeStruct(node_feats.shape, F32),
        ),
        in_specs=[hbm, hbm, inside, inside, inside] + [hbm] * 6,
        out_specs=(inside, inside),
        scratch_shapes=scratch,
        compiler_params=pltpu.CompilerParams(
            collective_id=0, has_side_effects=True, vmem_limit_bytes=VMEM_LIMIT
        ),
        name="edge_conv",
    )(node_feats, cotangent, wigner, sources.reshape(1, edges), dests, *weights)


def solution(mesh):
    node = P(None, "irrep", ("groups", "node"))
    edge = P(("groups", "node"))
    in_specs = (node, node, P(None, ("groups", "node")), edge, edge, edge) + (P(),) * 6
    return jax.shard_map(
        functools.partial(local, mesh.shape["node"], mesh.shape["irrep"]),
        mesh=mesh,
        in_specs=in_specs,
        out_specs=(node, node),
        check_vma=False,
    )
```

```python
import functools

import jax
import jax.numpy as jnp
from jax import lax
from jax.experimental import pallas as pl
from jax.experimental.pallas import tpu as pltpu
from jax.sharding import PartitionSpec as P

LMAX = 6
MMAX = 2
COEF = (LMAX + 1) ** 2
EDGE_SCALE = 0.5
F32 = jnp.float32
BF16 = jnp.bfloat16
MESH = pl.DeviceIdType.MESH
VMEM_LIMIT = 60 * 1024 * 1024

BASE = [0]
WOFF = [0]
for _l in range(LMAX + 1):
    _rows = 2 * min(_l, MMAX) + 1
    BASE.append(BASE[-1] + _rows)
    WOFF.append(WOFF[-1] + _rows * (2 * _l + 1))
ROWS = BASE[-1]

PARTS = ((6, 7), (5, 6), (4, 5), (0, 3), (3, 4))
BACK_PARTS = ((0, 1, 2), (4, 3))
BACK_DEGREES = (range(4, LMAX + 1), range(0, 4))


def frow(degree, order):
    return BASE[degree] + order + min(degree, MMAX)


def coef_rows(part):
    low, high = PARTS[part]
    return low * low, high * high - low * low


def frame_rows(part):
    low, high = PARTS[part]
    return BASE[low], BASE[high] - BASE[low]


def rotate_in(src, dst, wig, degrees, channels, edges, wig_base):
    halves = channels // 16

    def body(step, carry):
        tile = step // halves
        half = step % halves
        lanes = pl.ds(pl.multiple_of(tile * 128, 128), 128)
        wig_lanes = pl.ds(pl.multiple_of(wig_base + tile * 128, 128), 128)
        chans = pl.ds(pl.multiple_of(half * 16, 16), 16)
        for degree in degrees:
            cols = 2 * degree + 1
            parts = [src[degree * degree + c, chans, lanes].astype(F32) for c in range(cols)]
            for r in range(2 * min(degree, MMAX) + 1):
                at = WOFF[degree] + r * cols
                total = wig[at : at + 1, wig_lanes] * parts[0]
                for c in range(1, cols):
                    total = total + wig[at + c : at + c + 1, wig_lanes] * parts[c]
                dst[BASE[degree] + r, chans, lanes] = total.astype(BF16)
        return carry

    lax.fori_loop(0, (edges // 128) * halves, body, 0)


def rotate_out(src, dst, wig, degrees, channels, edges, wig_base):
    halves = channels // 16

    def body(step, carry):
        tile = step // halves
        half = step % halves
        lanes = pl.ds(pl.multiple_of(tile * 128, 128), 128)
        wig_lanes = pl.ds(pl.multiple_of(wig_base + tile * 128, 128), 128)
        chans = pl.ds(pl.multiple_of(half * 16, 16), 16)
        for degree in degrees:
            cols = 2 * degree + 1
            count = 2 * min(degree, MMAX) + 1
            parts = [src[BASE[degree] + r, chans, lanes].astype(F32) for r in range(count)]
            for c in range(cols):
                at = WOFF[degree] + c
                total = wig[at : at + 1, wig_lanes] * parts[0]
                for r in range(1, count):
                    at = WOFF[degree] + r * cols + c
                    total = total + wig[at : at + 1, wig_lanes] * parts[r]
                dst[degree * degree + c, chans, lanes] = total.astype(BF16)
        return carry

    lax.fori_loop(0, (edges // 128) * halves, body, 0)


def dot_nn(a, b):
    return jnp.dot(a, b, preferred_element_type=F32)


def dot_tn(a, b):
    return lax.dot_general(a, b, (((0,), (0,)), ((), ())), preferred_element_type=F32)


def dot_nt(a, b):
    return lax.dot_general(a, b, (((1,), (1,)), ((), ())), preferred_element_type=F32)


def mix(weights, frame, out, transposed, dtype, wanted=range(LMAX + 1)):
    zero, one, two = weights
    width, share = frame.shape[1], frame.shape[2]
    dot = dot_tn if transposed else dot_nn

    def pick(ref, lead, degrees, low):
        span = pl.ds((degrees[0] - low) * width, len(degrees) * width)
        return ref[(*lead, slice(None), span) if transposed else (*lead, span, slice(None))]

    rows = jnp.concatenate([frame[frow(l, 0)] for l in range(LMAX + 1)], axis=0)
    res = dot(pick(zero, (), wanted, 0), rows)
    for at, l in enumerate(wanted):
        out[frow(l, 0)] = res[at * width : (at + 1) * width].astype(dtype)
    for order, mat in ((1, one), (2, two)):
        degrees = [l for l in wanted if l >= order]
        rows = jnp.concatenate(
            [
                jnp.concatenate([frame[frow(l, order)], frame[frow(l, -order)]], axis=1)
                for l in range(order, LMAX + 1)
            ],
            axis=0,
        )
        real = dot(pick(mat, (0,), degrees, order), rows)
        imag = dot(pick(mat, (1,), degrees, order), rows)
        if transposed:
            plus = real[:, :share] + imag[:, share:]
            minus = real[:, share:] - imag[:, :share]
        else:
            plus = real[:, :share] - imag[:, share:]
            minus = imag[:, :share] + real[:, share:]
        for at, l in enumerate(degrees):
            out[frow(l, order)] = plus[at * width : (at + 1) * width].astype(dtype)
            out[frow(l, -order)] = minus[at * width : (at + 1) * width].astype(dtype)


def kernel(
    n_node,
    n_irrep,
    node_hbm,
    cot_hbm,
    wig_in,
    sources,
    dests,
    fz_hbm,
    fo_hbm,
    ft_hbm,
    sz_hbm,
    so_hbm,
    st_hbm,
    update,
    grad,
    fz,
    fo,
    ft,
    sz,
    so,
    st,
    wig,
    src_table,
    dst_table,
    nodes_all,
    cot_all,
    src_rows,
    seed_rows,
    frame_out,
    frame_in,
    seed_frame,
    hidden,
    back_gate,
    gated,
    back_hidden,
    back_frame,
    back_in,
    upd_out,
    pair_in,
    upd_mid,
    upd_in,
    grad_out,
    grad_in,
    grad_acc,
    load_sem,
    local_sem,
    node_send,
    node_recv,
    cot_send,
    cot_recv,
    fr_send,
    fr_recv,
    bk_send,
    bk_recv,
    up_send,
    up_recv,
    gr_send,
    gr_recv,
):
    group = lax.axis_index("groups")
    me_n = lax.axis_index("node")
    me_i = lax.axis_index("irrep")
    chans, atoms = node_hbm.shape[1], node_hbm.shape[2]
    width = chans * n_irrep
    edges = sources.shape[1]
    share = edges // n_irrep
    all_atoms = atoms * n_node

    n_chip = n_irrep // 2
    chip, core = me_i // 2, lax.rem(me_i, 2)

    def node_peer(k):
        return (group, lax.rem(me_n + k, n_node), me_i)

    def at_node(n):
        return (group, n, me_i)

    def in_line(n):
        return jnp.logical_and(n >= 0, n < n_node)

    def chip_of(k):
        return lax.rem(chip + k, n_chip)

    def chans_of(i):
        return pl.ds(pl.multiple_of(i * chans, chans), chans)

    def atoms_of(n):
        return pl.ds(pl.multiple_of(n * atoms, atoms), atoms)

    def irrep_peer(k):
        return (group, me_n, lax.rem(me_i + k, n_irrep))

    loads = [
        pltpu.make_async_copy(a, b, load_sem.at[i])
        for i, (a, b) in enumerate(
            ((fz_hbm, fz), (fo_hbm, fo), (ft_hbm, ft), (sz_hbm, sz), (so_hbm, so), (st_hbm, st))
        )
    ]

    barrier = pltpu.get_barrier_semaphore()
    for k in range(1, n_node):
        pl.semaphore_signal(barrier, inc=1, device_id=node_peer(k), device_id_type=MESH)
    for k in range(1, n_irrep):
        pl.semaphore_signal(barrier, inc=1, device_id=irrep_peer(k), device_id_type=MESH)
    pl.semaphore_wait(barrier, n_node + n_irrep - 2)

    sends = []

    def remote(src, dst, send, recv, peer):
        copy = pltpu.make_async_remote_copy(
            src_ref=src,
            dst_ref=dst,
            send_sem=send,
            recv_sem=recv,
            device_id=peer,
            device_id_type=MESH,
        )
        copy.start()
        sends.append(copy)
        return copy

    line_sends = []

    def line_copy(src, dst, send, recv, peer):
        return pltpu.make_async_remote_copy(
            src_ref=src,
            dst_ref=dst,
            send_sem=send,
            recv_sem=recv,
            device_id=peer,
            device_id_type=MESH,
        )

    def line_send(cond, *spec):
        @pl.when(cond)
        def _():
            line_copy(*spec).start()

        line_sends.append((cond, spec))

    my_atoms = pl.ds(pl.multiple_of(me_n * atoms, atoms), atoms)
    my_chans = pl.ds(pl.multiple_of(me_i * chans, chans), chans)
    my_share = pl.multiple_of(me_i * share, share)
    my_edges = pl.ds(my_share, share)

    for part in range(len(PARTS)):
        at, count = coef_rows(part)
        for dist in (2, 1):
            for way, sign in ((0, 1), (1, -1)):
                line_send(
                    in_line(me_n + sign * dist),
                    node_hbm.at[pl.ds(at, count)],
                    nodes_all.at[pl.ds(at, count), :, my_atoms],
                    node_send.at[part, way, dist - 1],
                    node_recv.at[part, way, dist - 1],
                    at_node(me_n + sign * dist),
                )
    beside = (group, me_n, chip * 2 + 1 - core)

    def cot_step(src, hop, k, owner, peer):
        return remote(
            src, cot_all.at[:, chans_of(owner), :], cot_send.at[hop, k], cot_recv.at[hop, k], peer
        )

    cot_copies = [
        cot_step(cot_hbm, 0, k, me_i, (group, me_n, chip_of(k) * 2 + core))
        for k in range(1, n_chip)
    ]
    cot_near = [cot_step(cot_hbm, 0, 0, me_i, beside)]
    own_node = pltpu.make_async_copy(node_hbm, nodes_all.at[:, :, my_atoms], local_sem.at[0])
    own_cot = pltpu.make_async_copy(cot_hbm, cot_all.at[:, my_chans, :], local_sem.at[1])
    own_node.start()
    own_cot.start()
    for copy in loads:
        copy.start()

    wig[...] = wig_in[...].astype(F32)

    def fill(i, carry):
        at = pl.multiple_of(i * 128, 128)
        rows = lax.broadcasted_iota(jnp.int32, (128, edges), 0) + i * 128
        src_table[pl.ds(at, 128), :] = jnp.where(rows == sources[...], 1.0, 0.0).astype(BF16)
        return carry

    lax.fori_loop(0, all_atoms // 128, fill, 0)
    rows = lax.broadcasted_iota(jnp.int32, (atoms, share), 0)
    dst_table[...] = jnp.where(rows == dests[:, my_edges], 1.0, 0.0).astype(BF16)

    own_cot.wait()
    for k, copy in enumerate(cot_copies, 1):
        copy.wait_recv()
        owner = chip_of(n_chip - k) * 2 + core
        cot_near.append(cot_step(cot_all.at[:, chans_of(owner), :], 1, k, owner, beside))
    for copy in cot_near:
        copy.wait_recv()

    def seed(i, carry):
        cot = cot_all[pl.ds(i * 7, 7)].reshape(7 * width, atoms)
        got = dot_nn(cot, dst_table[...]).astype(BF16)
        seed_rows[pl.ds(i * 7, 7)] = got.reshape(7, width, share)
        return carry

    lax.fori_loop(0, COEF // 7, seed, 0)
    rotate_in(seed_rows, seed_frame, wig, range(LMAX + 1), width, share, my_share)

    own_node.wait()
    frame_copies = []
    own_frames = []
    for part in range(len(PARTS)):
        at, count = coef_rows(part)
        for dist in (2, 1, *range(3, n_node)):
            for way, sign in ((0, 1), (1, -1)):
                here = nodes_all.at[pl.ds(at, count), :, atoms_of(me_n - sign * dist)]

                @pl.when(in_line(me_n - sign * dist))
                def _(here=here, way=way, sign=sign, dist=dist, part=part):
                    line_copy(
                        here,
                        here,
                        node_send.at[part, way, dist - 1],
                        node_recv.at[part, way, dist - 1],
                        at_node(me_n - sign * dist),
                    ).wait_recv()

                if 2 <= dist < n_node - 1:
                    line_send(
                        jnp.logical_and(in_line(me_n - sign * dist), in_line(me_n + sign)),
                        here,
                        here,
                        node_send.at[part, way, dist],
                        node_recv.at[part, way, dist],
                        at_node(me_n + sign),
                    )

        def gather(i, carry, at=at, count=count):
            lanes = pl.ds(pl.multiple_of(i * 256, 256), 256)
            tab = nodes_all[pl.ds(at, count)].reshape(count * chans, all_atoms)
            got = dot_nn(tab, src_table[:, lanes]).astype(BF16)
            src_rows[pl.ds(at, count), :, lanes] = got.reshape(count, chans, 256)
            return carry

        lax.fori_loop(0, edges // 256, gather, 0)
        rotate_in(src_rows, frame_out, wig, range(*PARTS[part]), chans, edges, 0)
        at, count = frame_rows(part)
        sent = []
        for k in range(1, n_irrep):
            peer = lax.rem(me_i + k, n_irrep)
            lanes = pl.ds(pl.multiple_of(peer * share, share), share)
            sent.append(
                remote(
                    frame_out.at[pl.ds(at, count), :, lanes],
                    frame_in.at[pl.ds(at, count), my_chans, :],
                    fr_send.at[part, k - 1],
                    fr_recv.at[part, k - 1],
                    irrep_peer(k),
                )
            )
        frame_copies.append(sent)
        own = pltpu.make_async_copy(
            frame_out.at[pl.ds(at, count), :, my_edges],
            frame_in.at[pl.ds(at, count), my_chans, :],
            local_sem.at[2 + part],
        )
        own.start()
        own_frames.append(own)

    for copy in loads:
        copy.wait()
    first = (fz, fo, ft)
    second = (sz, so, st)
    mix(second, seed_frame, back_gate, True, F32)
    for part in range(len(PARTS)):
        own_frames[part].wait()
        for copy in frame_copies[part]:
            copy.wait_recv()
    mix(first, frame_in, hidden, False, F32)

    def gate(i, carry):
        rows16 = pl.ds(pl.multiple_of(i * 16, 16), 16)
        s = hidden[0, rows16, :]
        g = jax.nn.sigmoid(s)
        total = jnp.zeros_like(s)
        gated[0, rows16, :] = (s * g).astype(BF16)
        for r in range(1, ROWS):
            h = hidden[r, rows16, :]
            b = back_gate[r, rows16, :]
            total = total + b * h
            gated[r, rows16, :] = (h * g).astype(BF16)
            back_hidden[r, rows16, :] = (b * g).astype(BF16)
        top = back_gate[0, rows16, :] * g * (1.0 + s * (1.0 - g)) + g * (1.0 - g) * total
        back_hidden[0, rows16, :] = top.astype(BF16)
        return carry

    lax.fori_loop(0, width // 16, gate, 0)

    back_copies = {}
    own_backs = {}
    for degrees, parts in zip(BACK_DEGREES, BACK_PARTS):
        mix(first, back_hidden, back_frame, True, BF16, degrees)
        for part in parts:
            at, count = frame_rows(part)
            back_copies[part] = [
                remote(
                    back_frame.at[pl.ds(at, count), chans_of(lax.rem(me_i + k, n_irrep)), :],
                    back_in.at[pl.ds(at, count), :, my_edges],
                    bk_send.at[part, k - 1],
                    bk_recv.at[part, k - 1],
                    irrep_peer(k),
                )
                for k in range(1, n_irrep)
            ]
            own_backs[part] = pltpu.make_async_copy(
                back_frame.at[pl.ds(at, count), my_chans, :],
                back_in.at[pl.ds(at, count), :, my_edges],
                local_sem.at[2 + len(PARTS) + part],
            )
            own_backs[part].start()

    def grad_spread(part):
        own_backs[part].wait()
        for copy in back_copies[part]:
            copy.wait_recv()
        rotate_out(back_in, src_rows, wig, range(*PARTS[part]), chans, edges, 0)
        at, count = coef_rows(part)

        def spread(i, carry, at=at, count=count):
            tab = src_table[pl.ds(pl.multiple_of(i * 2 * atoms, 2 * atoms), 2 * atoms), :]
            got = dot_nt(src_rows[pl.ds(at, count)].reshape(count * chans, edges), tab)
            got = got.astype(BF16)
            for j in range(2):
                piece = got[:, j * atoms : (j + 1) * atoms].reshape(count, chans, atoms)
                grad_out[2 * i + j, pl.ds(at, count)] = piece
            return carry

        lax.fori_loop(0, n_node // 2, spread, 0)

    def grad_send(part, way, sign, dist, cond):
        at, count = coef_rows(part)
        rows = pl.ds(at, count)
        owner = me_n + sign * dist
        near = dist <= 2
        line_send(
            jnp.logical_and(cond, in_line(owner)),
            grad_out.at[owner, rows],
            grad_in.at[way, dist - 1, rows] if near else grad_acc.at[way, dist - 3, rows],
            gr_send.at[part, way, dist - 1],
            gr_recv.at[part, way, dist - 1],
            at_node(owner if near else me_n + sign),
        )

    def grad_first(part):
        for dist in range(n_node - 1, 0, -1):
            for way, sign in ((0, 1), (1, -1)):
                alone = dist == 1 or dist == n_node - 1
                grad_send(part, way, sign, dist, True if alone else ~in_line(me_n - sign))

    def grad_later(part):
        at, count = coef_rows(part)
        for dist in range(n_node - 2, 1, -1):
            for way, sign in ((0, 1), (1, -1)):
                owner = me_n + sign * dist
                cond = jnp.logical_and(in_line(me_n - sign), in_line(owner))
                here = grad_acc.at[way, dist - 2, pl.ds(at, count)]

                @pl.when(cond)
                def _(here=here, way=way, sign=sign, dist=dist, owner=owner):
                    line_copy(
                        here,
                        here,
                        gr_send.at[part, way, dist],
                        gr_recv.at[part, way, dist],
                        at_node(me_n - sign),
                    ).wait_recv()

                    def add(i, carry):
                        more = grad_acc[way, dist - 2, i].astype(F32)
                        grad_out[owner, i] = (grad_out[owner, i].astype(F32) + more).astype(BF16)
                        return carry

                    lax.fori_loop(at, at + count, add, 0)

                grad_send(part, way, sign, dist, in_line(me_n - sign))

    message, sent_rows = seed_frame, seed_rows
    mix(second, gated, message, False, BF16)
    order = [part for parts in BACK_PARTS for part in parts]
    grad_spread(order[0])
    grad_first(order[0])
    rotate_out(message, sent_rows, wig, range(LMAX + 1), width, share, my_share)

    def aggregate(i, carry):
        rows7 = sent_rows[pl.ds(i * 7, 7)].reshape(7 * width, share)
        got = dot_nt(rows7, dst_table[...]).astype(BF16)
        upd_out[pl.ds(i * 7, 7)] = got.reshape(7, width, atoms)
        return carry

    lax.fori_loop(0, COEF // 7, aggregate, 0)
    pair_copies = [
        remote(
            upd_out.at[:, chans_of(chip_of(k) * 2 + 1 - core), :],
            pair_in.at[k],
            up_send.at[0, k],
            up_recv.at[0, k],
            beside,
        )
        for k in range(n_chip)
    ]
    grad_later(order[0])
    grad_spread(order[1])
    grad_first(order[1])
    for copy in pair_copies:
        copy.wait_recv()
    upd_copies = []
    for k in range(1, n_chip):

        def pair_sum(i, carry, k=k):
            mine = upd_out[i, chans_of(chip_of(k) * 2 + core), :].astype(F32)
            upd_mid[k - 1, i] = (mine + pair_in[k, i].astype(F32)).astype(BF16)
            return carry

        lax.fori_loop(0, COEF, pair_sum, 0)
        upd_copies.append(
            remote(
                upd_mid.at[k - 1],
                upd_in.at[k - 1],
                up_send.at[1, k],
                up_recv.at[1, k],
                (group, me_n, chip_of(k) * 2 + core),
            )
        )
    grad_later(order[1])
    for part in order[2:]:
        grad_spread(part)
        grad_first(part)
        grad_later(part)

    for copy in upd_copies:
        copy.wait_recv()

    def finish_update(i, carry):
        total = upd_out[i, my_chans, :].astype(F32) + pair_in[0, i].astype(F32)
        for k in range(n_chip - 1):
            total = total + upd_in[k, i].astype(F32)
        update[i] = (EDGE_SCALE * total).astype(BF16)
        return carry

    lax.fori_loop(0, COEF, finish_update, 0)

    for part in order:
        at, count = coef_rows(part)
        rows = pl.ds(at, count)
        for way, sign in ((0, 1), (1, -1)):
            for dist in (1, 2):
                there = in_line(me_n - sign * dist)
                here = grad_in.at[way, dist - 1, rows]

                @pl.when(there)
                def _(here=here, way=way, sign=sign, dist=dist, part=part):
                    line_copy(
                        here,
                        here,
                        gr_send.at[part, way, dist - 1],
                        gr_recv.at[part, way, dist - 1],
                        at_node(me_n - sign * dist),
                    ).wait_recv()

                @pl.when(jnp.logical_not(there))
                def _(way=way, dist=dist, rows=rows, count=count):
                    grad_in[way, dist - 1, rows] = jnp.zeros((count, chans, atoms), BF16)

        def finish_grad(i, carry):
            total = grad_out[me_n, i].astype(F32)
            for way in range(2):
                for dist in range(2):
                    total = total + grad_in[way, dist, i].astype(F32)
            grad[i] = EDGE_SCALE * total
            return carry

        lax.fori_loop(at, at + count, finish_grad, 0)

    for cond, spec in line_sends:

        @pl.when(cond)
        def _(spec=spec):
            line_copy(*spec).wait_send()

    for copy in sends:
        copy.wait_send()


def local(
    n_node,
    n_irrep,
    node_feats,
    cotangent,
    wigner,
    sources,
    targets,
    counts,
    first_zero,
    first_one,
    first_two,
    second_zero,
    second_one,
    second_two,
):
    coefs, chans, atoms = node_feats.shape
    edges = sources.shape[0]
    share = edges // n_irrep
    width = chans * n_irrep
    blocks = counts.shape[0]
    slot = jnp.arange(edges // blocks, dtype=jnp.int32)
    live = (slot[None, :] < counts[:, None]).reshape(edges)
    dests = jnp.where(live, targets - lax.axis_index("node") * atoms, -1).reshape(1, edges)
    weights = (first_zero, first_one, first_two, second_zero, second_one, second_two)
    parts = len(PARTS)
    n_chip = n_irrep // 2
    vmem = pltpu.VMEM
    dma = pltpu.SemaphoreType.DMA
    frame = (ROWS, width, share)
    scratch = [vmem(w.shape, BF16) for w in weights] + [
        vmem(wigner.shape, F32),
        vmem((atoms * n_node, edges), BF16),
        vmem((atoms, share), BF16),
        vmem((coefs, chans, atoms * n_node), BF16),
        vmem((coefs, width, atoms), BF16),
        vmem((coefs, chans, edges), BF16),
        vmem((coefs, width, share), BF16),
        vmem((ROWS, chans, edges), BF16),
        vmem(frame, BF16),
        vmem(frame, BF16),
        vmem(frame, F32),
        vmem(frame, F32),
        vmem(frame, BF16),
        vmem(frame, BF16),
        vmem(frame, BF16),
        vmem((ROWS, chans, edges), BF16),
        vmem((coefs, width, atoms), BF16),
        vmem((n_chip, coefs, chans, atoms), BF16),
        vmem((n_chip - 1, coefs, chans, atoms), BF16),
        vmem((n_chip - 1, coefs, chans, atoms), BF16),
        vmem((n_node, coefs, chans, atoms), BF16),
        vmem((2, 2, coefs, chans, atoms), BF16),
        vmem((2, n_node - 3, coefs, chans, atoms), BF16),
        dma((len(weights),)),
        dma((2 + 2 * parts,)),
        dma((parts, 2, n_node - 1)),
        dma((parts, 2, n_node - 1)),
        dma((2, n_chip)),
        dma((2, n_chip)),
        dma((parts, n_irrep - 1)),
        dma((parts, n_irrep - 1)),
        dma((parts, n_irrep - 1)),
        dma((parts, n_irrep - 1)),
        dma((2, n_chip)),
        dma((2, n_chip)),
        dma((parts, 2, n_node - 1)),
        dma((parts, 2, n_node - 1)),
    ]
    hbm = pl.BlockSpec(memory_space=pl.ANY)
    inside = pl.BlockSpec(memory_space=pltpu.VMEM)
    return pl.pallas_call(
        functools.partial(kernel, n_node, n_irrep),
        out_shape=(
            jax.ShapeDtypeStruct(node_feats.shape, BF16),
            jax.ShapeDtypeStruct(node_feats.shape, F32),
        ),
        in_specs=[hbm, hbm, inside, inside, inside] + [hbm] * 6,
        out_specs=(inside, inside),
        scratch_shapes=scratch,
        compiler_params=pltpu.CompilerParams(
            collective_id=0, has_side_effects=True, vmem_limit_bytes=VMEM_LIMIT
        ),
        name="edge_conv",
    )(node_feats, cotangent, wigner, sources.reshape(1, edges), dests, *weights)


def solution(mesh):
    node = P(None, "irrep", ("groups", "node"))
    edge = P(("groups", "node"))
    in_specs = (node, node, P(None, ("groups", "node")), edge, edge, edge) + (P(),) * 6
    return jax.shard_map(
        functools.partial(local, mesh.shape["node"], mesh.shape["irrep"]),
        mesh=mesh,
        in_specs=in_specs,
        out_specs=(node, node),
        check_vma=False,
    )
```

```python
import functools

import jax
import jax.numpy as jnp
from jax import lax
from jax.experimental import pallas as pl
from jax.experimental.pallas import tpu as pltpu
from jax.sharding import PartitionSpec as P

LMAX = 6
MMAX = 2
COEF = (LMAX + 1) ** 2
EDGE_SCALE = 0.5
F32 = jnp.float32
BF16 = jnp.bfloat16
MESH = pl.DeviceIdType.MESH
VMEM_LIMIT = 60 * 1024 * 1024

BASE = [0]
WOFF = [0]
for _l in range(LMAX + 1):
    _rows = 2 * min(_l, MMAX) + 1
    BASE.append(BASE[-1] + _rows)
    WOFF.append(WOFF[-1] + _rows * (2 * _l + 1))
ROWS = BASE[-1]

PARTS = ((6, 7), (5, 6), (4, 5), (0, 3), (3, 4))
BACK_PARTS = ((0, 1, 2), (4, 3))
BACK_DEGREES = (range(4, LMAX + 1), range(0, 4))


def frow(degree, order):
    return BASE[degree] + order + min(degree, MMAX)


def coef_rows(part):
    low, high = PARTS[part]
    return low * low, high * high - low * low


def frame_rows(part):
    low, high = PARTS[part]
    return BASE[low], BASE[high] - BASE[low]


def rotate_in(src, dst, wig, degrees, channels, edges, wig_base):
    halves = channels // 16

    def body(step, carry):
        tile = step // halves
        half = step % halves
        lanes = pl.ds(pl.multiple_of(tile * 128, 128), 128)
        wig_lanes = pl.ds(pl.multiple_of(wig_base + tile * 128, 128), 128)
        chans = pl.ds(pl.multiple_of(half * 16, 16), 16)
        for degree in degrees:
            cols = 2 * degree + 1
            parts = [src[degree * degree + c, chans, lanes].astype(F32) for c in range(cols)]
            for r in range(2 * min(degree, MMAX) + 1):
                at = WOFF[degree] + r * cols
                total = wig[at : at + 1, wig_lanes] * parts[0]
                for c in range(1, cols):
                    total = total + wig[at + c : at + c + 1, wig_lanes] * parts[c]
                dst[BASE[degree] + r, chans, lanes] = total.astype(BF16)
        return carry

    lax.fori_loop(0, (edges // 128) * halves, body, 0)


def rotate_out(src, dst, wig, degrees, channels, edges, wig_base):
    halves = channels // 16

    def body(step, carry):
        tile = step // halves
        half = step % halves
        lanes = pl.ds(pl.multiple_of(tile * 128, 128), 128)
        wig_lanes = pl.ds(pl.multiple_of(wig_base + tile * 128, 128), 128)
        chans = pl.ds(pl.multiple_of(half * 16, 16), 16)
        for degree in degrees:
            cols = 2 * degree + 1
            count = 2 * min(degree, MMAX) + 1
            parts = [src[BASE[degree] + r, chans, lanes].astype(F32) for r in range(count)]
            for c in range(cols):
                at = WOFF[degree] + c
                total = wig[at : at + 1, wig_lanes] * parts[0]
                for r in range(1, count):
                    at = WOFF[degree] + r * cols + c
                    total = total + wig[at : at + 1, wig_lanes] * parts[r]
                dst[degree * degree + c, chans, lanes] = total.astype(BF16)
        return carry

    lax.fori_loop(0, (edges // 128) * halves, body, 0)


def dot_nn(a, b):
    return jnp.dot(a, b, preferred_element_type=F32)


def dot_tn(a, b):
    return lax.dot_general(a, b, (((0,), (0,)), ((), ())), preferred_element_type=F32)


def dot_nt(a, b):
    return lax.dot_general(a, b, (((1,), (1,)), ((), ())), preferred_element_type=F32)


def mix(weights, frame, out, transposed, dtype, wanted=range(LMAX + 1)):
    zero, one, two = weights
    width, share = frame.shape[1], frame.shape[2]
    dot = dot_tn if transposed else dot_nn

    def pick(ref, lead, degrees, low):
        span = pl.ds((degrees[0] - low) * width, len(degrees) * width)
        return ref[(*lead, slice(None), span) if transposed else (*lead, span, slice(None))]

    rows = jnp.concatenate([frame[frow(l, 0)] for l in range(LMAX + 1)], axis=0)
    res = dot(pick(zero, (), wanted, 0), rows)
    for at, l in enumerate(wanted):
        out[frow(l, 0)] = res[at * width : (at + 1) * width].astype(dtype)
    for order, mat in ((1, one), (2, two)):
        degrees = [l for l in wanted if l >= order]
        rows = jnp.concatenate(
            [
                jnp.concatenate([frame[frow(l, order)], frame[frow(l, -order)]], axis=1)
                for l in range(order, LMAX + 1)
            ],
            axis=0,
        )
        real = dot(pick(mat, (0,), degrees, order), rows)
        imag = dot(pick(mat, (1,), degrees, order), rows)
        if transposed:
            plus = real[:, :share] + imag[:, share:]
            minus = real[:, share:] - imag[:, :share]
        else:
            plus = real[:, :share] - imag[:, share:]
            minus = imag[:, :share] + real[:, share:]
        for at, l in enumerate(degrees):
            out[frow(l, order)] = plus[at * width : (at + 1) * width].astype(dtype)
            out[frow(l, -order)] = minus[at * width : (at + 1) * width].astype(dtype)


def kernel(
    n_node,
    n_irrep,
    node_hbm,
    cot_hbm,
    wig_in,
    sources,
    dests,
    fz_hbm,
    fo_hbm,
    ft_hbm,
    sz_hbm,
    so_hbm,
    st_hbm,
    update,
    grad,
    fz,
    fo,
    ft,
    sz,
    so,
    st,
    wig,
    src_table,
    dst_table,
    nodes_all,
    cot_all,
    src_rows,
    seed_rows,
    frame_out,
    frame_in,
    seed_frame,
    hidden,
    back_gate,
    gated,
    back_hidden,
    back_frame,
    back_in,
    upd_out,
    pair_in,
    upd_mid,
    upd_in,
    grad_out,
    grad_in,
    grad_acc,
    load_sem,
    local_sem,
    node_send,
    node_recv,
    cot_send,
    cot_recv,
    fr_send,
    fr_recv,
    bk_send,
    bk_recv,
    up_send,
    up_recv,
    gr_send,
    gr_recv,
):
    group = lax.axis_index("groups")
    me_n = lax.axis_index("node")
    me_i = lax.axis_index("irrep")
    chans, atoms = node_hbm.shape[1], node_hbm.shape[2]
    width = chans * n_irrep
    edges = sources.shape[1]
    share = edges // n_irrep
    all_atoms = atoms * n_node

    n_chip = n_irrep // 2
    chip, core = me_i // 2, lax.rem(me_i, 2)

    def node_peer(k):
        return (group, lax.rem(me_n + k, n_node), me_i)

    def at_node(n):
        return (group, n, me_i)

    def in_line(n):
        return jnp.logical_and(n >= 0, n < n_node)

    def chip_of(k):
        return lax.rem(chip + k, n_chip)

    def chans_of(i):
        return pl.ds(pl.multiple_of(i * chans, chans), chans)

    def atoms_of(n):
        return pl.ds(pl.multiple_of(n * atoms, atoms), atoms)

    def irrep_peer(k):
        return (group, me_n, lax.rem(me_i + k, n_irrep))

    loads = [
        pltpu.make_async_copy(a, b, load_sem.at[i])
        for i, (a, b) in enumerate(
            ((fz_hbm, fz), (fo_hbm, fo), (ft_hbm, ft), (sz_hbm, sz), (so_hbm, so), (st_hbm, st))
        )
    ]

    barrier = pltpu.get_barrier_semaphore()
    for k in range(1, n_node):
        pl.semaphore_signal(barrier, inc=1, device_id=node_peer(k), device_id_type=MESH)
    for k in range(1, n_irrep):
        pl.semaphore_signal(barrier, inc=1, device_id=irrep_peer(k), device_id_type=MESH)
    pl.semaphore_wait(barrier, n_node + n_irrep - 2)

    sends = []

    def remote(src, dst, send, recv, peer):
        copy = pltpu.make_async_remote_copy(
            src_ref=src,
            dst_ref=dst,
            send_sem=send,
            recv_sem=recv,
            device_id=peer,
            device_id_type=MESH,
        )
        copy.start()
        sends.append(copy)
        return copy

    line_sends = []

    def line_copy(src, dst, send, recv, peer):
        return pltpu.make_async_remote_copy(
            src_ref=src,
            dst_ref=dst,
            send_sem=send,
            recv_sem=recv,
            device_id=peer,
            device_id_type=MESH,
        )

    def line_send(cond, *spec):
        @pl.when(cond)
        def _():
            line_copy(*spec).start()

        line_sends.append((cond, spec))

    my_atoms = pl.ds(pl.multiple_of(me_n * atoms, atoms), atoms)
    my_chans = pl.ds(pl.multiple_of(me_i * chans, chans), chans)
    my_share = pl.multiple_of(me_i * share, share)
    my_edges = pl.ds(my_share, share)

    for part in range(len(PARTS)):
        at, count = coef_rows(part)
        for dist in (2, 1):
            for way, sign in ((0, 1), (1, -1)):
                line_send(
                    in_line(me_n + sign * dist),
                    node_hbm.at[pl.ds(at, count)],
                    nodes_all.at[pl.ds(at, count), :, my_atoms],
                    node_send.at[part, way, dist - 1],
                    node_recv.at[part, way, dist - 1],
                    at_node(me_n + sign * dist),
                )
    beside = (group, me_n, chip * 2 + 1 - core)

    def cot_step(src, hop, k, owner, peer):
        return remote(
            src, cot_all.at[:, chans_of(owner), :], cot_send.at[hop, k], cot_recv.at[hop, k], peer
        )

    cot_copies = [
        cot_step(cot_hbm, 0, k, me_i, (group, me_n, chip_of(k) * 2 + core))
        for k in range(1, n_chip)
    ]
    cot_near = [cot_step(cot_hbm, 0, 0, me_i, beside)]
    own_node = pltpu.make_async_copy(node_hbm, nodes_all.at[:, :, my_atoms], local_sem.at[0])
    own_cot = pltpu.make_async_copy(cot_hbm, cot_all.at[:, my_chans, :], local_sem.at[1])
    own_node.start()
    own_cot.start()
    for copy in loads:
        copy.start()

    wig[...] = wig_in[...].astype(F32)

    def fill(i, carry):
        at = pl.multiple_of(i * 128, 128)
        rows = lax.broadcasted_iota(jnp.int32, (128, edges), 0) + i * 128
        src_table[pl.ds(at, 128), :] = jnp.where(rows == sources[...], 1.0, 0.0).astype(BF16)
        return carry

    lax.fori_loop(0, all_atoms // 128, fill, 0)
    rows = lax.broadcasted_iota(jnp.int32, (atoms, share), 0)
    dst_table[...] = jnp.where(rows == dests[:, my_edges], 1.0, 0.0).astype(BF16)

    own_node.wait()
    frame_copies = []
    own_frames = []
    for part in range(len(PARTS)):
        at, count = coef_rows(part)
        for dist in (2, 1, *range(3, n_node)):
            for way, sign in ((0, 1), (1, -1)):
                here = nodes_all.at[pl.ds(at, count), :, atoms_of(me_n - sign * dist)]

                @pl.when(in_line(me_n - sign * dist))
                def _(here=here, way=way, sign=sign, dist=dist, part=part):
                    line_copy(
                        here,
                        here,
                        node_send.at[part, way, dist - 1],
                        node_recv.at[part, way, dist - 1],
                        at_node(me_n - sign * dist),
                    ).wait_recv()

                if 2 <= dist < n_node - 1:
                    line_send(
                        jnp.logical_and(in_line(me_n - sign * dist), in_line(me_n + sign)),
                        here,
                        here,
                        node_send.at[part, way, dist],
                        node_recv.at[part, way, dist],
                        at_node(me_n + sign),
                    )

        def gather(i, carry, at=at, count=count):
            lanes = pl.ds(pl.multiple_of(i * 256, 256), 256)
            tab = nodes_all[pl.ds(at, count)].reshape(count * chans, all_atoms)
            got = dot_nn(tab, src_table[:, lanes]).astype(BF16)
            src_rows[pl.ds(at, count), :, lanes] = got.reshape(count, chans, 256)
            return carry

        lax.fori_loop(0, edges // 256, gather, 0)
        rotate_in(src_rows, frame_out, wig, range(*PARTS[part]), chans, edges, 0)
        at, count = frame_rows(part)
        sent = []
        for k in range(1, n_irrep):
            peer = lax.rem(me_i + k, n_irrep)
            lanes = pl.ds(pl.multiple_of(peer * share, share), share)
            sent.append(
                remote(
                    frame_out.at[pl.ds(at, count), :, lanes],
                    frame_in.at[pl.ds(at, count), my_chans, :],
                    fr_send.at[part, k - 1],
                    fr_recv.at[part, k - 1],
                    irrep_peer(k),
                )
            )
        frame_copies.append(sent)
        own = pltpu.make_async_copy(
            frame_out.at[pl.ds(at, count), :, my_edges],
            frame_in.at[pl.ds(at, count), my_chans, :],
            local_sem.at[2 + part],
        )
        own.start()
        own_frames.append(own)

    own_cot.wait()
    for k, copy in enumerate(cot_copies, 1):
        copy.wait_recv()
        owner = chip_of(n_chip - k) * 2 + core
        cot_near.append(cot_step(cot_all.at[:, chans_of(owner), :], 1, k, owner, beside))
    for copy in cot_near:
        copy.wait_recv()

    def seed(i, carry):
        cot = cot_all[pl.ds(i * 7, 7)].reshape(7 * width, atoms)
        got = dot_nn(cot, dst_table[...]).astype(BF16)
        seed_rows[pl.ds(i * 7, 7)] = got.reshape(7, width, share)
        return carry

    lax.fori_loop(0, COEF // 7, seed, 0)
    rotate_in(seed_rows, seed_frame, wig, range(LMAX + 1), width, share, my_share)

    for copy in loads:
        copy.wait()
    first = (fz, fo, ft)
    second = (sz, so, st)
    mix(second, seed_frame, back_gate, True, F32)
    for part in range(len(PARTS)):
        own_frames[part].wait()
        for copy in frame_copies[part]:
            copy.wait_recv()
    mix(first, frame_in, hidden, False, F32)

    def gate(i, carry):
        rows16 = pl.ds(pl.multiple_of(i * 16, 16), 16)
        s = hidden[0, rows16, :]
        g = jax.nn.sigmoid(s)
        total = jnp.zeros_like(s)
        gated[0, rows16, :] = (s * g).astype(BF16)
        for r in range(1, ROWS):
            h = hidden[r, rows16, :]
            b = back_gate[r, rows16, :]
            total = total + b * h
            gated[r, rows16, :] = (h * g).astype(BF16)
            back_hidden[r, rows16, :] = (b * g).astype(BF16)
        top = back_gate[0, rows16, :] * g * (1.0 + s * (1.0 - g)) + g * (1.0 - g) * total
        back_hidden[0, rows16, :] = top.astype(BF16)
        return carry

    lax.fori_loop(0, width // 16, gate, 0)

    back_copies = {}
    own_backs = {}
    for degrees, parts in zip(BACK_DEGREES, BACK_PARTS):
        mix(first, back_hidden, back_frame, True, BF16, degrees)
        for part in parts:
            at, count = frame_rows(part)
            back_copies[part] = [
                remote(
                    back_frame.at[pl.ds(at, count), chans_of(lax.rem(me_i + k, n_irrep)), :],
                    back_in.at[pl.ds(at, count), :, my_edges],
                    bk_send.at[part, k - 1],
                    bk_recv.at[part, k - 1],
                    irrep_peer(k),
                )
                for k in range(1, n_irrep)
            ]
            own_backs[part] = pltpu.make_async_copy(
                back_frame.at[pl.ds(at, count), my_chans, :],
                back_in.at[pl.ds(at, count), :, my_edges],
                local_sem.at[2 + len(PARTS) + part],
            )
            own_backs[part].start()

    def grad_spread(part):
        own_backs[part].wait()
        for copy in back_copies[part]:
            copy.wait_recv()
        rotate_out(back_in, src_rows, wig, range(*PARTS[part]), chans, edges, 0)
        at, count = coef_rows(part)

        def spread(i, carry, at=at, count=count):
            tab = src_table[pl.ds(pl.multiple_of(i * 2 * atoms, 2 * atoms), 2 * atoms), :]
            got = dot_nt(src_rows[pl.ds(at, count)].reshape(count * chans, edges), tab)
            got = got.astype(BF16)
            for j in range(2):
                piece = got[:, j * atoms : (j + 1) * atoms].reshape(count, chans, atoms)
                grad_out[2 * i + j, pl.ds(at, count)] = piece
            return carry

        lax.fori_loop(0, n_node // 2, spread, 0)

    def grad_send(part, way, sign, dist, cond):
        at, count = coef_rows(part)
        rows = pl.ds(at, count)
        owner = me_n + sign * dist
        near = dist <= 2
        line_send(
            jnp.logical_and(cond, in_line(owner)),
            grad_out.at[owner, rows],
            grad_in.at[way, dist - 1, rows] if near else grad_acc.at[way, dist - 3, rows],
            gr_send.at[part, way, dist - 1],
            gr_recv.at[part, way, dist - 1],
            at_node(owner if near else me_n + sign),
        )

    def grad_first(part):
        for dist in range(n_node - 1, 0, -1):
            for way, sign in ((0, 1), (1, -1)):
                alone = dist == 1 or dist == n_node - 1
                grad_send(part, way, sign, dist, True if alone else ~in_line(me_n - sign))

    def grad_later(part):
        at, count = coef_rows(part)
        for dist in range(n_node - 2, 1, -1):
            for way, sign in ((0, 1), (1, -1)):
                owner = me_n + sign * dist
                cond = jnp.logical_and(in_line(me_n - sign), in_line(owner))
                here = grad_acc.at[way, dist - 2, pl.ds(at, count)]

                @pl.when(cond)
                def _(here=here, way=way, sign=sign, dist=dist, owner=owner):
                    line_copy(
                        here,
                        here,
                        gr_send.at[part, way, dist],
                        gr_recv.at[part, way, dist],
                        at_node(me_n - sign),
                    ).wait_recv()

                    def add(i, carry):
                        more = grad_acc[way, dist - 2, i].astype(F32)
                        grad_out[owner, i] = (grad_out[owner, i].astype(F32) + more).astype(BF16)
                        return carry

                    lax.fori_loop(at, at + count, add, 0)

                grad_send(part, way, sign, dist, in_line(me_n - sign))

    message, sent_rows = seed_frame, seed_rows
    mix(second, gated, message, False, BF16)
    order = [part for parts in BACK_PARTS for part in parts]
    grad_spread(order[0])
    grad_first(order[0])
    rotate_out(message, sent_rows, wig, range(LMAX + 1), width, share, my_share)

    def aggregate(i, carry):
        rows7 = sent_rows[pl.ds(i * 7, 7)].reshape(7 * width, share)
        got = dot_nt(rows7, dst_table[...]).astype(BF16)
        upd_out[pl.ds(i * 7, 7)] = got.reshape(7, width, atoms)
        return carry

    lax.fori_loop(0, COEF // 7, aggregate, 0)
    pair_copies = [
        remote(
            upd_out.at[:, chans_of(chip_of(k) * 2 + 1 - core), :],
            pair_in.at[k],
            up_send.at[0, k],
            up_recv.at[0, k],
            beside,
        )
        for k in range(n_chip)
    ]
    grad_later(order[0])
    grad_spread(order[1])
    grad_first(order[1])
    for copy in pair_copies:
        copy.wait_recv()
    upd_copies = []
    for k in range(1, n_chip):

        def pair_sum(i, carry, k=k):
            mine = upd_out[i, chans_of(chip_of(k) * 2 + core), :].astype(F32)
            upd_mid[k - 1, i] = (mine + pair_in[k, i].astype(F32)).astype(BF16)
            return carry

        lax.fori_loop(0, COEF, pair_sum, 0)
        upd_copies.append(
            remote(
                upd_mid.at[k - 1],
                upd_in.at[k - 1],
                up_send.at[1, k],
                up_recv.at[1, k],
                (group, me_n, chip_of(k) * 2 + core),
            )
        )
    grad_later(order[1])
    for part in order[2:]:
        grad_spread(part)
        grad_first(part)
        grad_later(part)

    for copy in upd_copies:
        copy.wait_recv()

    def finish_update(i, carry):
        total = upd_out[i, my_chans, :].astype(F32) + pair_in[0, i].astype(F32)
        for k in range(n_chip - 1):
            total = total + upd_in[k, i].astype(F32)
        update[i] = (EDGE_SCALE * total).astype(BF16)
        return carry

    lax.fori_loop(0, COEF, finish_update, 0)

    for part in order:
        at, count = coef_rows(part)
        rows = pl.ds(at, count)
        for way, sign in ((0, 1), (1, -1)):
            for dist in (1, 2):
                there = in_line(me_n - sign * dist)
                here = grad_in.at[way, dist - 1, rows]

                @pl.when(there)
                def _(here=here, way=way, sign=sign, dist=dist, part=part):
                    line_copy(
                        here,
                        here,
                        gr_send.at[part, way, dist - 1],
                        gr_recv.at[part, way, dist - 1],
                        at_node(me_n - sign * dist),
                    ).wait_recv()

                @pl.when(jnp.logical_not(there))
                def _(way=way, dist=dist, rows=rows, count=count):
                    grad_in[way, dist - 1, rows] = jnp.zeros((count, chans, atoms), BF16)

        def finish_grad(i, carry):
            total = grad_out[me_n, i].astype(F32)
            for way in range(2):
                for dist in range(2):
                    total = total + grad_in[way, dist, i].astype(F32)
            grad[i] = EDGE_SCALE * total
            return carry

        lax.fori_loop(at, at + count, finish_grad, 0)

    for cond, spec in line_sends:

        @pl.when(cond)
        def _(spec=spec):
            line_copy(*spec).wait_send()

    for copy in sends:
        copy.wait_send()


def local(
    n_node,
    n_irrep,
    node_feats,
    cotangent,
    wigner,
    sources,
    targets,
    counts,
    first_zero,
    first_one,
    first_two,
    second_zero,
    second_one,
    second_two,
):
    coefs, chans, atoms = node_feats.shape
    edges = sources.shape[0]
    share = edges // n_irrep
    width = chans * n_irrep
    blocks = counts.shape[0]
    slot = jnp.arange(edges // blocks, dtype=jnp.int32)
    live = (slot[None, :] < counts[:, None]).reshape(edges)
    dests = jnp.where(live, targets - lax.axis_index("node") * atoms, -1).reshape(1, edges)
    weights = (first_zero, first_one, first_two, second_zero, second_one, second_two)
    parts = len(PARTS)
    n_chip = n_irrep // 2
    vmem = pltpu.VMEM
    dma = pltpu.SemaphoreType.DMA
    frame = (ROWS, width, share)
    scratch = [vmem(w.shape, BF16) for w in weights] + [
        vmem(wigner.shape, F32),
        vmem((atoms * n_node, edges), BF16),
        vmem((atoms, share), BF16),
        vmem((coefs, chans, atoms * n_node), BF16),
        vmem((coefs, width, atoms), BF16),
        vmem((coefs, chans, edges), BF16),
        vmem((coefs, width, share), BF16),
        vmem((ROWS, chans, edges), BF16),
        vmem(frame, BF16),
        vmem(frame, BF16),
        vmem(frame, F32),
        vmem(frame, F32),
        vmem(frame, BF16),
        vmem(frame, BF16),
        vmem(frame, BF16),
        vmem((ROWS, chans, edges), BF16),
        vmem((coefs, width, atoms), BF16),
        vmem((n_chip, coefs, chans, atoms), BF16),
        vmem((n_chip - 1, coefs, chans, atoms), BF16),
        vmem((n_chip - 1, coefs, chans, atoms), BF16),
        vmem((n_node, coefs, chans, atoms), BF16),
        vmem((2, 2, coefs, chans, atoms), BF16),
        vmem((2, n_node - 3, coefs, chans, atoms), BF16),
        dma((len(weights),)),
        dma((2 + 2 * parts,)),
        dma((parts, 2, n_node - 1)),
        dma((parts, 2, n_node - 1)),
        dma((2, n_chip)),
        dma((2, n_chip)),
        dma((parts, n_irrep - 1)),
        dma((parts, n_irrep - 1)),
        dma((parts, n_irrep - 1)),
        dma((parts, n_irrep - 1)),
        dma((2, n_chip)),
        dma((2, n_chip)),
        dma((parts, 2, n_node - 1)),
        dma((parts, 2, n_node - 1)),
    ]
    hbm = pl.BlockSpec(memory_space=pl.ANY)
    inside = pl.BlockSpec(memory_space=pltpu.VMEM)
    return pl.pallas_call(
        functools.partial(kernel, n_node, n_irrep),
        out_shape=(
            jax.ShapeDtypeStruct(node_feats.shape, BF16),
            jax.ShapeDtypeStruct(node_feats.shape, F32),
        ),
        in_specs=[hbm, hbm, inside, inside, inside] + [hbm] * 6,
        out_specs=(inside, inside),
        scratch_shapes=scratch,
        compiler_params=pltpu.CompilerParams(
            collective_id=0, has_side_effects=True, vmem_limit_bytes=VMEM_LIMIT
        ),
        name="edge_conv",
    )(node_feats, cotangent, wigner, sources.reshape(1, edges), dests, *weights)


def solution(mesh):
    node = P(None, "irrep", ("groups", "node"))
    edge = P(("groups", "node"))
    in_specs = (node, node, P(None, ("groups", "node")), edge, edge, edge) + (P(),) * 6
    return jax.shard_map(
        functools.partial(local, mesh.shape["node"], mesh.shape["irrep"]),
        mesh=mesh,
        in_specs=in_specs,
        out_specs=(node, node),
        check_vma=False,
    )
```
